32 devices in a mesh: groups: 2 (over y), dp: 16 (over z, x, core).
Axes of the slice: x: 2, y: 2, z: 4, core: 2. Of those that a mesh axis runs over, the one named last changes fastest.
Arguments:
- node_rows: bfloat16 [16384, 8192], P(('groups', 'dp')), parts along dimension 0, may hold values from -6 to 6
- kept_counts: int32 [64], P(('groups', 'dp')), parts along dimension 0, may hold values from 8 to 256, as said below
- parents: int32 [64, 256], P(('groups', 'dp')), parts along dimension 0, may hold values from 0 to 254, as said below
- cache_len: int32 [64], P(('groups', 'dp')), parts along dimension 0, may hold values from 128 to 1024
- cache_kv: bfloat16 [64, 2, 1024, 128], P(('groups', 'dp')), parts along dimension 0, may hold values from -480 to 480
- norm_gain: float32 [8192], replicated, may hold values from 0.5 to 2
- w_qkv: bfloat16 [8192, 1280], P('dp'), may hold values from -0.0625 to 0.0625
- b_qkv: float32 [1280], replicated, may hold values from -3 to 3
Outputs:
- attended: bfloat16 [16384, 1024], P(('groups', 'dp')), parts along dimension 0
The draws below stay inside these ranges and needn't reach their ends.
There are 2 independent parts, one for each index of `groups`. The reference program is written for one: setup_inputs(seed, part) draws one part's arguments, and reference() takes and returns one part's arrays. A program takes and returns all parts, laid end to end along the dimension named above; an argument that names none is the same for every part. Nothing has to cross between parts.
Inputs may be any that keep to these rules, and one draw needn't show every extreme that they name: The counts of one part add up to exactly 3072; on some device every request keeps 256 nodes. The kept nodes of request r are its first kept_counts[r] slots. parents[r, 0] = 0, and 0 <= parents[r, i] < i for i >= 1.
All inputs are finite; a program needn't handle non-finite values.
Results may differ from the reference program's by a relative error of at most 0.0045.
The reference program's roundings to bfloat16 on the way count: a program that leaves them out, or rounds other values in their place, can miss the bound.
Values may be sent and summed in bfloat16 or wider, within the bound.
No kernel may reach another device: no remote copies, remote signals or barrier semaphores. Data moves between devices by JAX's collectives and lax.ppermute only.
A program may use at most 128 MiB of HBM per device.

```python
import math
import jax
import jax.numpy as jnp
from jax import lax

D = 8192
HEAD = 128
GROUP = 8
MAXN = 256
MEAN_NODES = 96
REQ_DEV = 2
CACHE = 1024
REQUESTS = 32
QKV = 1280


def draw_kept_counts(key, part):
    key = jax.random.fold_in(key, 11)
    spare_max = MAXN - 8
    first_key, second_key, third_key, fourth_key = jax.random.split(key, 4)
    heavy_dev = jax.random.randint(first_key, (), 0, REQUESTS // REQ_DEV)
    request_ids = jnp.arange(REQUESTS, dtype=jnp.int32)
    on_heavy = request_ids // REQ_DEV == heavy_dev
    roomy_req = jax.random.permutation(second_key, REQUESTS) < REQUESTS // 2
    capacity = jnp.where(roomy_req, spare_max, jax.random.randint(third_key, (REQUESTS,), 0, spare_max + 1))
    capacity = jnp.where(on_heavy, 0, capacity)
    needed = (MEAN_NODES - 8) * REQUESTS - REQ_DEV * spare_max
    ranking = jax.random.permutation(fourth_key, REQUESTS * spare_max).reshape(REQUESTS, spare_max)
    usable = jnp.arange(spare_max)[None, :] < capacity[:, None]
    ranking = jnp.where(usable, ranking, REQUESTS * spare_max)
    cutoff = jnp.sort(ranking.reshape(-1))[needed - 1]
    chosen = jnp.sum((ranking <= cutoff).astype(jnp.int32), axis=1)
    return jnp.where(on_heavy, MAXN, 8 + chosen).astype(jnp.int32)


def draw_parents(key, part):
    key = jax.random.fold_in(key, 12)
    positions = jnp.arange(MAXN, dtype=jnp.int32)
    drawn = jax.random.randint(key, (REQUESTS, MAXN), 0, jnp.maximum(positions, 1)[None, :]).astype(jnp.int32)
    return drawn.at[0, MAXN - 1].set(MAXN - 2).astype(jnp.int32)


def draw_cache_len(key, part):
    key = jax.random.fold_in(key, 13)
    first_key, second_key = jax.random.split(key)
    lengths = jax.random.randint(first_key, (REQUESTS,), CACHE // 8, CACHE + 1)
    picked = jax.random.randint(second_key, (), 0, REQUESTS)
    return jnp.where(jnp.arange(REQUESTS) == picked, CACHE, lengths).astype(jnp.int32)


def draw_cache_kv(key, part):
    key = jax.random.fold_in(key, 14)
    first_key = jax.random.fold_in(key, 0)
    values32 = jnp.clip(jax.random.normal(first_key, (REQUESTS, 2, CACHE, HEAD), jnp.float32), -6.0, 6.0)
    return values32.astype(jnp.bfloat16)


def levels(stream_key, shape, shards, smallest, high):
    def one(dim, parts):
        draws = jax.random.uniform(jax.random.fold_in(jax.random.fold_in(stream_key, 6), dim), (parts,), jnp.float32, smallest / len(shards), high / len(shards))
        return jnp.repeat(jnp.exp(draws), shape[dim] // parts).reshape((-1,) + (1,) * (len(shape) - dim - 1))

    factor_of = one(*shards[0])
    for cut in shards[1:]:
        factor_of = factor_of * one(*cut)
    return factor_of


def scatter_about(own_key, shape, deviation, bound, pieces=(), kind=jnp.bfloat16):
    factor_of = levels(own_key, shape, pieces, -0.22, 0.18) if pieces else 1.0
    result = jax.random.normal(own_key, shape, jnp.float32) * deviation * factor_of
    return jnp.minimum(jnp.maximum(result, -bound), bound).astype(kind)


def setup_inputs(seed: int = 0, part: int = 0) -> dict:
    keys = jax.random.split(jax.random.key(seed), 9)
    own_keys = jax.random.split(jax.random.fold_in(keys[8], part), 9)
    return {
        "node_rows": scatter_about(own_keys[0], (REQUESTS * MAXN, D), 1.0, 6.0, ((0, 16),)),
        "kept_counts": draw_kept_counts(jax.random.fold_in(jax.random.fold_in(keys[8], part), 71), part),
        "parents": draw_parents(jax.random.fold_in(jax.random.fold_in(keys[8], part), 71), part),
        "cache_len": draw_cache_len(jax.random.fold_in(jax.random.fold_in(keys[8], part), 71), part),
        "cache_kv": draw_cache_kv(jax.random.fold_in(jax.random.fold_in(keys[8], part), 71), part),
        "norm_gain": jnp.clip(jnp.exp(jax.random.uniform(keys[5], (D,), jnp.float32, math.log(0.5), math.log(2.0))), 0.5, 2.0),
        "w_qkv": scatter_about(keys[6], (D, QKV), D ** -0.5, 0.0625, ((0, 16),)),
        "b_qkv": scatter_about(keys[7], (QKV,), 0.5, 3.0, (), jnp.float32),
    }


EPSILON = 1e-06
ROPE_BASE = 1000000.0

def normalize(row_block, norm_gain):
    values32 = row_block.astype(jnp.float32)
    mean_square = lax.optimization_barrier(jnp.mean(values32 * values32, axis=-1, keepdims=True))
    return (values32 * lax.rsqrt(mean_square + EPSILON) * norm_gain).astype(jnp.bfloat16)

def ancestry(parent_row):
    max_nodes = parent_row.shape[0]
    positions = jnp.arange(max_nodes, dtype=jnp.int32)
    parent_link = (parent_row[:, None] == positions[None, :]) & (positions[:, None] >= 1)
    reached = (parent_link | (positions[:, None] == positions[None, :])).astype(jnp.bfloat16)
    for squaring in range((max_nodes - 1).bit_length()):
        reached = jnp.minimum(jnp.dot(reached, reached, preferred_element_type=jnp.float32), 1.0).astype(jnp.bfloat16)
    return reached

def spin(vectors, cosine, sine_part):
    half_size = vectors.shape[-1] // 2
    lower_half = vectors[..., :half_size]
    upper_half = vectors[..., half_size:]
    return jnp.concatenate([lower_half * cosine - upper_half * sine_part, upper_half * cosine + lower_half * sine_part], axis=-1)

def attend(bundle):
    projected, parent_row, kept_count, length, cache_pair = bundle
    max_nodes = projected.shape[0]
    reached = ancestry(parent_row)
    depth_of = lax.optimization_barrier(jnp.sum(reached.astype(jnp.float32), axis=1)) - 1.0
    placed = length.astype(jnp.float32) + depth_of
    frequency = ROPE_BASE ** (-(jnp.arange(HEAD // 2, dtype=jnp.float32) * 2.0 / HEAD))
    angles = placed[:, None] * frequency[None, :]
    cosine = jnp.cos(angles)
    sine_part = jnp.sin(angles)
    query_width = GROUP * HEAD
    queries = projected[:, :query_width].astype(jnp.float32).reshape(max_nodes, GROUP, HEAD)
    queries = spin(queries, cosine[:, None, :], sine_part[:, None, :]).astype(jnp.bfloat16)
    node_keys = spin(projected[:, query_width:query_width + HEAD].astype(jnp.float32), cosine, sine_part).astype(jnp.bfloat16)
    node_values = projected[:, query_width + HEAD:]
    scaling = HEAD ** (-0.5)
    queries32 = queries.astype(jnp.float32)
    past_scores = jnp.einsum('ngh,ch->ngc', queries32, cache_pair[0].astype(jnp.float32)) * scaling
    visible = jnp.arange(cache_pair.shape[1], dtype=jnp.int32) < length
    past_scores = jnp.where(visible[None, None, :], past_scores, -jnp.inf)
    tree_scores = jnp.einsum('ngh,mh->ngm', queries32, node_keys.astype(jnp.float32)) * scaling
    tree_scores = jnp.where(reached[:, None, :] > 0, tree_scores, -jnp.inf)
    row_top = jnp.maximum(lax.optimization_barrier(jnp.max(past_scores, axis=-1)), lax.optimization_barrier(jnp.max(tree_scores, axis=-1)))[..., None]
    past_weights = jnp.exp(past_scores - row_top)
    tree_weights = jnp.exp(tree_scores - row_top)
    denominator = lax.optimization_barrier(jnp.sum(past_weights, axis=-1, keepdims=True)) + lax.optimization_barrier(jnp.sum(tree_weights, axis=-1, keepdims=True))
    past_weights = (past_weights / denominator).astype(jnp.bfloat16)
    tree_weights = (tree_weights / denominator).astype(jnp.bfloat16)
    blended = jnp.einsum('ngc,ch->ngh', past_weights.astype(jnp.float32), cache_pair[1].astype(jnp.float32))
    blended = blended + jnp.einsum('ngm,mh->ngh', tree_weights.astype(jnp.float32), node_values.astype(jnp.float32))
    living = jnp.arange(max_nodes, dtype=jnp.int32) < kept_count
    blended = jnp.where(living[:, None, None], blended, 0.0)
    return blended.reshape(max_nodes, query_width).astype(jnp.bfloat16)

def reference(node_rows, kept_counts, parents, cache_len, cache_kv, norm_gain, w_qkv, b_qkv):
    row_ends = jnp.cumsum(kept_counts).astype(jnp.int32)
    starts = row_ends - kept_counts
    live_order = jnp.arange(MEAN_NODES * REQUESTS, dtype=jnp.int32)
    request_of = jnp.searchsorted(row_ends, live_order, side='right').astype(jnp.int32)
    node_of = live_order - starts[request_of]
    slot_rows = (request_of * MAXN + node_of).astype(jnp.int32)
    normed = normalize(node_rows[slot_rows], norm_gain)
    projected = (jnp.dot(normed, w_qkv, preferred_element_type=jnp.float32) + b_qkv).astype(jnp.bfloat16)
    padded = jnp.zeros((REQUESTS * MAXN, projected.shape[1]), jnp.bfloat16).at[slot_rows].set(projected)
    padded = padded.reshape(REQUESTS, MAXN, projected.shape[1])
    attended = lax.map(attend, (padded, parents, kept_counts, cache_len, cache_kv))
    return attended.reshape(REQUESTS * MAXN, GROUP * HEAD)
```

```python
import functools
import math

import jax
import jax.numpy as jnp
from jax import lax
from jax.experimental import pallas as pl
from jax.experimental.pallas import tpu as pltpu
from jax.sharding import PartitionSpec as P

HEAD = 128
GROUP = 8
EPSILON = 1e-06
ROPE_BASE = 1000000.0
SCORE_SCALE = HEAD ** (-0.5) * math.log2(math.e)
HEADS_PER_STEP = 2


def normalize(row_block, norm_gain):
    values32 = row_block.astype(jnp.float32)
    mean_square = jnp.mean(values32 * values32, axis=-1, keepdims=True)
    return (values32 * lax.rsqrt(mean_square + EPSILON) * norm_gain).astype(jnp.bfloat16)


def tree_tables(parents, cache_len):
    max_nodes = parents.shape[1]
    positions = jnp.arange(max_nodes, dtype=jnp.int32)
    parent_link = (parents[:, :, None] == positions) & (positions[:, None] >= 1)
    reached = (parent_link | (positions[:, None] == positions)).astype(jnp.bfloat16)
    for squaring in range((max_nodes - 1).bit_length()):
        product = jnp.einsum("rij,rjk->rik", reached, reached, preferred_element_type=jnp.float32)
        reached = jnp.minimum(product, 1.0).astype(jnp.bfloat16)
    depth_of = jnp.sum(reached.astype(jnp.float32), axis=2) - 1.0
    placed = cache_len.astype(jnp.float32)[:, None] + depth_of
    frequency = ROPE_BASE ** (-(jnp.arange(HEAD // 2, dtype=jnp.float32) * 2.0 / HEAD))
    angles = placed[:, :, None] * frequency
    cosine = jnp.cos(angles)
    sine_part = jnp.sin(angles)
    tree_bias = jnp.where(reached > 0, 0.0, -jnp.inf).astype(jnp.float32)
    return (
        tree_bias,
        jnp.concatenate([cosine, cosine], axis=-1),
        jnp.concatenate([-sine_part, sine_part], axis=-1),
    )


def project_kernel(x_ref, w_ref, b_ref, o_ref, acc_ref):
    step = pl.program_id(0)
    part = jnp.dot(x_ref[...], w_ref[...], preferred_element_type=jnp.float32)

    @pl.when(step == 0)
    def _():
        acc_ref[...] = part

    @pl.when(step > 0)
    def _():
        acc_ref[...] += part

    @pl.when(step == pl.num_programs(0) - 1)
    def _():
        o_ref[...] = (acc_ref[...] + b_ref[...]).astype(o_ref.dtype)


def project(normed, weights, bias):
    rows, depth = normed.shape
    columns = weights.shape[1]
    tile = 1024
    return pl.pallas_call(
        project_kernel,
        out_shape=jax.ShapeDtypeStruct((rows, columns), jnp.bfloat16),
        grid=(depth // tile,),
        in_specs=[
            pl.BlockSpec((rows, tile), lambda k: (0, k)),
            pl.BlockSpec((tile, columns), lambda k: (k, 0)),
            pl.BlockSpec((1, columns), lambda k: (0, 0)),
        ],
        out_specs=pl.BlockSpec((rows, columns), lambda k: (0, 0)),
        scratch_shapes=[pltpu.VMEM((rows, columns), jnp.float32)],
        compiler_params=pltpu.CompilerParams(vmem_limit_bytes=48 * 2**20),
        cost_estimate=pl.CostEstimate(
            flops=2 * rows * depth * columns,
            bytes_accessed=2 * (rows * depth + depth * columns + rows * columns),
            transcendentals=0,
        ),
    )(normed, weights, bias.reshape(1, columns))


def rotate(vectors, cosine, sine_part):
    return (vectors * cosine + pltpu.roll(vectors, HEAD // 2, 1) * sine_part).astype(jnp.bfloat16)


def attend_kernel(kept_ref, len_ref, q_ref, kv_ref, bias_ref, cos_ref, sin_ref, cache_ref, o_ref, key_ref):
    request = pl.program_id(0)
    cosine = cos_ref[0]
    sine_part = sin_ref[0]

    @pl.when(pl.program_id(1) == 0)
    def _():
        key_ref[...] = rotate(kv_ref[:, :HEAD].astype(jnp.float32), cosine, sine_part)

    max_nodes = q_ref.shape[0]
    cache = cache_ref.shape[2]
    past = lax.broadcasted_iota(jnp.int32, (1, cache), 1) < len_ref[request]
    past_bias = jnp.where(past, 0.0, -jnp.inf)
    living = lax.broadcasted_iota(jnp.int32, (max_nodes, 1), 0) < kept_ref[request]
    transposed = (((1,), (1,)), ((), ()))
    for head in range(q_ref.shape[1] // HEAD):
        columns = slice(head * HEAD, (head + 1) * HEAD)
        query = rotate(q_ref[:, columns].astype(jnp.float32), cosine, sine_part)
        past_scores = lax.dot_general(query, cache_ref[0, 0], transposed, preferred_element_type=jnp.float32)
        past_scores = past_scores * SCORE_SCALE + past_bias
        tree_scores = lax.dot_general(query, key_ref[...], transposed, preferred_element_type=jnp.float32)
        tree_scores = tree_scores * SCORE_SCALE + bias_ref[0]
        top = jnp.maximum(
            jnp.max(past_scores, axis=1, keepdims=True), jnp.max(tree_scores, axis=1, keepdims=True)
        )
        past_weights = jnp.exp2(past_scores - top)
        tree_weights = jnp.exp2(tree_scores - top)
        total = jnp.sum(past_weights, axis=1, keepdims=True) + jnp.sum(tree_weights, axis=1, keepdims=True)
        inverse = 1.0 / total
        blended = jnp.dot(
            (past_weights * inverse).astype(jnp.bfloat16), cache_ref[0, 1], preferred_element_type=jnp.float32
        )
        blended += jnp.dot(
            (tree_weights * inverse).astype(jnp.bfloat16), kv_ref[:, HEAD:], preferred_element_type=jnp.float32
        )
        o_ref[:, columns] = jnp.where(living, blended, 0.0).astype(o_ref.dtype)


def attend(projected, tree_bias, cosine, sine_part, kept_counts, cache_len, cache_kv):
    requests, max_nodes = tree_bias.shape[:2]
    cache = cache_kv.shape[2]
    width = HEADS_PER_STEP * HEAD
    table = pl.BlockSpec((1, max_nodes, HEAD), lambda r, h, *_: (r, 0, 0))
    return pl.pallas_call(
        attend_kernel,
        out_shape=jax.ShapeDtypeStruct((requests * max_nodes, GROUP * HEAD), jnp.bfloat16),
        grid_spec=pltpu.PrefetchScalarGridSpec(
            num_scalar_prefetch=2,
            grid=(requests, GROUP // HEADS_PER_STEP),
            in_specs=[
                pl.BlockSpec((max_nodes, width), lambda r, h, *_: (r, h)),
                pl.BlockSpec((max_nodes, 2 * HEAD), lambda r, h, *_: (r, GROUP // 2)),
                pl.BlockSpec((1, max_nodes, max_nodes), lambda r, h, *_: (r, 0, 0)),
                table,
                table,
                pl.BlockSpec((1, 2, cache, HEAD), lambda r, h, *_: (r, 0, 0, 0)),
            ],
            out_specs=pl.BlockSpec((max_nodes, width), lambda r, h, *_: (r, h)),
            scratch_shapes=[pltpu.VMEM((max_nodes, HEAD), jnp.bfloat16)],
        ),
        compiler_params=pltpu.CompilerParams(vmem_limit_bytes=40 * 2**20),
    )(kept_counts, cache_len, projected, projected, tree_bias, cosine, sine_part, cache_kv)


def on_device(node_rows, kept_counts, parents, cache_len, cache_kv, norm_gain, w_qkv, b_qkv):
    weights = lax.all_gather(w_qkv, "dp", axis=0, tiled=True)
    normed = normalize(node_rows, norm_gain)
    tables = tree_tables(parents, cache_len)
    normed, weights, tables = lax.optimization_barrier((normed, weights, tables))
    projected = project(normed, weights, b_qkv)
    return attend(projected, *tables, kept_counts, cache_len, cache_kv)


def solution(mesh):
    return jax.shard_map(
        on_device,
        mesh=mesh,
        in_specs=(
            P(("groups", "dp"), None),
            P(("groups", "dp")),
            P(("groups", "dp"), None),
            P(("groups", "dp")),
            P(("groups", "dp"), None, None, None),
            P(),
            P("dp", None),
            P(),
        ),
        out_specs=P(("groups", "dp"), None),
        check_vma=False,
    )
```

```python
import functools
import math

import jax
import jax.numpy as jnp
from jax import lax
from jax.experimental import pallas as pl
from jax.experimental.pallas import tpu as pltpu
from jax.sharding import PartitionSpec as P

HEAD = 128
GROUP = 8
EPSILON = 1e-06
ROPE_BASE = 1000000.0
SCORE_SCALE = HEAD ** (-0.5) * math.log2(math.e)
HEADS_PER_STEP = 2


def normalize(row_block, norm_gain):
    values32 = row_block.astype(jnp.float32)
    mean_square = jnp.mean(values32 * values32, axis=-1, keepdims=True)
    return (values32 * lax.rsqrt(mean_square + EPSILON) * norm_gain).astype(jnp.bfloat16)


def tree_tables(parents, cache_len):
    max_nodes = parents.shape[1]
    positions = jnp.arange(max_nodes, dtype=jnp.int32)
    parent_link = (parents[:, :, None] == positions) & (positions[:, None] >= 1)
    reached = (parent_link | (positions[:, None] == positions)).astype(jnp.bfloat16)
    for squaring in range((max_nodes - 1).bit_length()):
        product = jnp.einsum("rij,rjk->rik", reached, reached, preferred_element_type=jnp.float32)
        reached = jnp.minimum(product, 1.0).astype(jnp.bfloat16)
    depth_of = jnp.sum(reached.astype(jnp.float32), axis=2) - 1.0
    placed = cache_len.astype(jnp.float32)[:, None] + depth_of
    frequency = ROPE_BASE ** (-(jnp.arange(HEAD // 2, dtype=jnp.float32) * 2.0 / HEAD))
    angles = placed[:, :, None] * frequency
    cosine = jnp.cos(angles)
    sine_part = jnp.sin(angles)
    tree_bias = jnp.where(reached > 0, 0.0, -jnp.inf).astype(jnp.float32)
    return (
        tree_bias,
        jnp.concatenate([cosine, cosine], axis=-1),
        jnp.concatenate([-sine_part, sine_part], axis=-1),
    )


def project_kernel(x_ref, w_ref, b_ref, o_ref, acc_ref):
    step = pl.program_id(0)
    part = jnp.dot(x_ref[...], w_ref[...], preferred_element_type=jnp.float32)

    @pl.when(step == 0)
    def _():
        acc_ref[...] = part

    @pl.when(step > 0)
    def _():
        acc_ref[...] += part

    @pl.when(step == pl.num_programs(0) - 1)
    def _():
        o_ref[...] = (acc_ref[...] + b_ref[...]).astype(o_ref.dtype)


def project(normed, weights, bias):
    rows, depth = normed.shape
    columns = weights.shape[1]
    tile = 1024
    return pl.pallas_call(
        project_kernel,
        out_shape=jax.ShapeDtypeStruct((rows, columns), jnp.bfloat16),
        grid=(depth // tile,),
        in_specs=[
            pl.BlockSpec((rows, tile), lambda k: (0, k)),
            pl.BlockSpec((tile, columns), lambda k: (k, 0)),
            pl.BlockSpec((1, columns), lambda k: (0, 0)),
        ],
        out_specs=pl.BlockSpec((rows, columns), lambda k: (0, 0)),
        scratch_shapes=[pltpu.VMEM((rows, columns), jnp.float32)],
        compiler_params=pltpu.CompilerParams(vmem_limit_bytes=60 * 2**20),
        cost_estimate=pl.CostEstimate(
            flops=2 * rows * depth * columns,
            bytes_accessed=2 * (rows * depth + depth * columns + rows * columns),
            transcendentals=0,
        ),
    )(normed, weights, bias.reshape(1, columns))


def rotate(vectors, cosine, sine_part):
    return (vectors * cosine + pltpu.roll(vectors, HEAD // 2, 1) * sine_part).astype(jnp.bfloat16)


def attend_kernel(kept_ref, len_ref, q_ref, kv_ref, bias_ref, cos_ref, sin_ref, cache_ref, o_ref, key_ref):
    request = pl.program_id(0)
    cosine = cos_ref[0]
    sine_part = sin_ref[0]

    @pl.when(pl.program_id(1) == 0)
    def _():
        key_ref[...] = rotate(kv_ref[:, :HEAD].astype(jnp.float32), cosine, sine_part)

    max_nodes = q_ref.shape[0]
    cache = cache_ref.shape[2]
    past = lax.broadcasted_iota(jnp.int32, (1, cache), 1) < len_ref[request]
    past_bias = jnp.where(past, 0.0, -jnp.inf)
    living = lax.broadcasted_iota(jnp.int32, (max_nodes, 1), 0) < kept_ref[request]
    transposed = (((1,), (1,)), ((), ()))
    for head in range(q_ref.shape[1] // HEAD):
        columns = slice(head * HEAD, (head + 1) * HEAD)
        query = rotate(q_ref[:, columns].astype(jnp.float32), cosine, sine_part)
        past_scores = lax.dot_general(query, cache_ref[0, 0], transposed, preferred_element_type=jnp.float32)
        past_scores = past_scores * SCORE_SCALE + past_bias
        tree_scores = lax.dot_general(query, key_ref[...], transposed, preferred_element_type=jnp.float32)
        tree_scores = tree_scores * SCORE_SCALE + bias_ref[0]
        top = jnp.maximum(
            jnp.max(past_scores, axis=1, keepdims=True), jnp.max(tree_scores, axis=1, keepdims=True)
        )
        past_weights = jnp.exp2(past_scores - top)
        tree_weights = jnp.exp2(tree_scores - top)
        total = jnp.sum(past_weights, axis=1, keepdims=True) + jnp.sum(tree_weights, axis=1, keepdims=True)
        inverse = 1.0 / total
        blended = jnp.dot(
            (past_weights * inverse).astype(jnp.bfloat16), cache_ref[0, 1], preferred_element_type=jnp.float32
        )
        blended += jnp.dot(
            (tree_weights * inverse).astype(jnp.bfloat16), kv_ref[:, HEAD:], preferred_element_type=jnp.float32
        )
        o_ref[:, columns] = jnp.where(living, blended, 0.0).astype(o_ref.dtype)


def attend(projected, tree_bias, cosine, sine_part, kept_counts, cache_len, cache_kv):
    requests, max_nodes = tree_bias.shape[:2]
    cache = cache_kv.shape[2]
    width = HEADS_PER_STEP * HEAD
    table = pl.BlockSpec((1, max_nodes, HEAD), lambda r, h, *_: (r, 0, 0))
    return pl.pallas_call(
        attend_kernel,
        out_shape=jax.ShapeDtypeStruct((requests * max_nodes, GROUP * HEAD), jnp.bfloat16),
        grid_spec=pltpu.PrefetchScalarGridSpec(
            num_scalar_prefetch=2,
            grid=(requests, GROUP // HEADS_PER_STEP),
            in_specs=[
                pl.BlockSpec((max_nodes, width), lambda r, h, *_: (r, h)),
                pl.BlockSpec((max_nodes, 2 * HEAD), lambda r, h, *_: (r, GROUP // 2)),
                pl.BlockSpec((1, max_nodes, max_nodes), lambda r, h, *_: (r, 0, 0)),
                table,
                table,
                pl.BlockSpec((1, 2, cache, HEAD), lambda r, h, *_: (r, 0, 0, 0)),
            ],
            out_specs=pl.BlockSpec((max_nodes, width), lambda r, h, *_: (r, h)),
            scratch_shapes=[pltpu.VMEM((max_nodes, HEAD), jnp.bfloat16)],
        ),
        compiler_params=pltpu.CompilerParams(vmem_limit_bytes=60 * 2**20),
    )(kept_counts, cache_len, projected, projected, tree_bias, cosine, sine_part, cache_kv)


def norm_kernel(steps, core_ref, x_ref, other_ref, gain_ref, w_ref, *refs):
    out_ref, copy_ref = refs[-2:]
    copy_ref[...] = w_ref[...]

    def work(rows_ref):
        values32 = rows_ref[...].astype(jnp.float32)
        mean_square = jnp.mean(values32 * values32, axis=-1, keepdims=True)
        factor = lax.rsqrt(mean_square + EPSILON)
        width = rows_ref.shape[1] // (2 * CHIPS)
        for chip in range(CHIPS):
            source = pl.ds(pl.multiple_of((2 * chip + core_ref[0]) * width, width), width)
            block = rows_ref[:, source].astype(jnp.float32) * factor * gain_ref[:, source]
            out_ref[:, chip * width : (chip + 1) * width] = block.astype(jnp.bfloat16)

    pl.when(pl.program_id(0) < steps)(lambda: work(x_ref))
    pl.when(pl.program_id(0) >= steps)(lambda: work(other_ref))


def normalize_both(own_rows, other_rows, norm_gain, core, columns, unread):
    rows, depth = own_rows.shape
    tile = 128
    steps = rows // tile
    copy_spec = pl.BlockSpec((columns.shape[0] // (2 * steps), columns.shape[1]), lambda r, *_: (r, 0))
    return pl.pallas_call(
        functools.partial(norm_kernel, steps),
        out_shape=(
            jax.ShapeDtypeStruct((2 * rows, depth // 2), jnp.bfloat16),
            jax.ShapeDtypeStruct(columns.shape, columns.dtype),
        ),
        grid_spec=pltpu.PrefetchScalarGridSpec(
            num_scalar_prefetch=1,
            grid=(2 * steps,),
            in_specs=[
                pl.BlockSpec((tile, depth), lambda r, *_: (jnp.minimum(r, steps - 1), 0)),
                pl.BlockSpec((tile, depth), lambda r, *_: (jnp.maximum(r - steps, 0), 0)),
                pl.BlockSpec((1, depth), lambda r, *_: (0, 0)),
                copy_spec,
                *[pl.BlockSpec(memory_space=pl.ANY)] * len(unread),
            ],
            out_specs=(pl.BlockSpec((tile, depth // 2), lambda r, *_: (r, 0)), copy_spec),
        ),
        compiler_params=pltpu.CompilerParams(vmem_limit_bytes=NORM_LIMIT * 2**20),
        cost_estimate=pl.CostEstimate(flops=8 * rows * depth, bytes_accessed=6 * rows * depth, transcendentals=0),
    )(core.reshape(1), own_rows, other_rows, norm_gain.reshape(1, depth), columns, *unread)


def accumulate_kernel(count, unread, first, steps, copies, place_ref, *refs):
    refs = refs[: 2 * count] + refs[2 * count + unread :]
    if copies:
        refs[-1][...] = refs[2 * count][...]
        refs = refs[: 2 * count] + refs[2 * count + 1 : -1]
    x_refs, piece_refs, rest = refs[:count], refs[count : 2 * count], refs[2 * count :]

    def side(which):
        total = None if first else rest[which][...]
        for x_ref, w_ref in zip(x_refs, piece_refs):
            part = jnp.dot(x_ref[...], w_ref[...], preferred_element_type=jnp.float32)
            total = part if total is None else total + part
        rest[which if first else 2 + which][...] = total

    pl.when(pl.program_id(0) < steps)(lambda: side(1))
    pl.when(pl.program_id(0) >= steps)(lambda: side(0))


def accumulate(normed, pieces, sums, copied=None, unread=()):
    rows = normed.shape[0] // 2
    columns = pieces[0][0].shape[1]
    tile = 256
    steps = rows // tile
    count = len(pieces)
    depth = sum(array.shape[0] for array, _ in pieces)
    places = jnp.stack([place for _, place in pieces]).astype(jnp.int32)

    def rows_spec(index):
        return pl.BlockSpec(
            (tile, pieces[index][0].shape[0]), lambda r, place_ref: (lax.rem(r + steps, 2 * steps), place_ref[index])
        )

    sum_specs = (
        pl.BlockSpec((tile, columns), lambda r, *_: (jnp.maximum(r - steps, 0), 0)),
        pl.BlockSpec((tile, columns), lambda r, *_: (jnp.minimum(r, steps - 1), 0)),
    )
    out = jax.ShapeDtypeStruct((rows, columns), jnp.float32)
    first = sums is None
    extra = [] if copied is None else [copied]
    copy_specs = [pl.BlockSpec((array.shape[0] // (2 * steps), array.shape[1]), lambda r, *_: (r, 0)) for array in extra]
    return pl.pallas_call(
        functools.partial(accumulate_kernel, count, len(unread), first, steps, bool(extra)),
        out_shape=(out, out, *[jax.ShapeDtypeStruct(array.shape, array.dtype) for array in extra]),
        grid_spec=pltpu.PrefetchScalarGridSpec(
            num_scalar_prefetch=1,
            grid=(2 * steps,),
            in_specs=[rows_spec(i) for i in range(count)]
            + [pl.BlockSpec(array.shape, lambda r, *_: (0, 0)) for array, _ in pieces]
            + [pl.BlockSpec(memory_space=pl.ANY)] * len(unread)
            + copy_specs
            + ([] if first else list(sum_specs)),
            out_specs=(*sum_specs, *copy_specs),
        ),
        input_output_aliases={} if first else {1 + 2 * count + len(unread) + len(extra) + i: i for i in range(2)},
        compiler_params=pltpu.CompilerParams(vmem_limit_bytes=DOT_LIMIT * 2**20),
        cost_estimate=pl.CostEstimate(
            flops=4 * rows * depth * columns,
            bytes_accessed=4 * rows * depth + 2 * depth * columns + (8 if first else 16) * rows * columns,
            transcendentals=0,
        ),
    )(places, *([normed] * count), *[array for array, _ in pieces], *unread, *extra, *(() if first else sums))


def softmax_values(query, past_keys, past_values, past_bias, node_keys, node_values, tree_bias, living):
    transposed = (((1,), (1,)), ((), ()))
    past_scores = lax.dot_general(query, past_keys, transposed, preferred_element_type=jnp.float32)
    past_scores = past_scores * SCORE_SCALE + past_bias
    tree_scores = lax.dot_general(query, node_keys, transposed, preferred_element_type=jnp.float32)
    tree_scores = tree_scores * SCORE_SCALE + tree_bias
    top = jnp.maximum(jnp.max(past_scores, axis=1, keepdims=True), jnp.max(tree_scores, axis=1, keepdims=True))
    past_weights = jnp.exp2(past_scores - top)
    tree_weights = jnp.exp2(tree_scores - top)
    total = jnp.sum(past_weights, axis=1, keepdims=True) + jnp.sum(tree_weights, axis=1, keepdims=True)
    inverse = 1.0 / total
    blended = jnp.dot((past_weights * inverse).astype(jnp.bfloat16), past_values, preferred_element_type=jnp.float32)
    blended += jnp.dot((tree_weights * inverse).astype(jnp.bfloat16), node_values, preferred_element_type=jnp.float32)
    return jnp.where(living, blended, 0.0).astype(jnp.bfloat16)


def masks(kept_ref, len_ref, request, max_nodes, cache):
    past = lax.broadcasted_iota(jnp.int32, (1, cache), 1) < len_ref[request]
    living = lax.broadcasted_iota(jnp.int32, (max_nodes, 1), 0) < kept_ref[request]
    return jnp.where(past, 0.0, -jnp.inf), living


def heads_kernel(kept_ref, len_ref, own_b, got_b, own_a, got_a, b_ref, bias_ref, cos_ref, sin_ref, cache_ref, o_ref):
    past_bias, living = masks(kept_ref, len_ref, pl.program_id(0), own_a.shape[0], cache_ref.shape[2])
    cosine, sine_part = cos_ref[0], sin_ref[0]

    def column_block(index):
        own_ref, got_ref, start = (own_b, got_b, 0) if index * HEAD < SPLIT else (own_a, got_a, SPLIT)
        columns = slice(index * HEAD - start, (index + 1) * HEAD - start)
        bias = b_ref[:, index * HEAD : (index + 1) * HEAD]
        return (own_ref[:, columns] + got_ref[:, columns] + bias).astype(jnp.bfloat16)

    node_keys = rotate(column_block(GROUP).astype(jnp.float32), cosine, sine_part)
    node_values = column_block(GROUP + 1)
    for head in reversed(range(GROUP)):
        query = rotate(column_block(head).astype(jnp.float32), cosine, sine_part)
        o_ref[:, head * HEAD : (head + 1) * HEAD] = softmax_values(
            query, cache_ref[0, 0], cache_ref[0, 1], past_bias, node_keys, node_values, bias_ref[0], living
        )


def attend_sums(parts, bias, tables, kept_counts, cache_len, cache_kv):
    requests, max_nodes = tables[0].shape[:2]
    cache = cache_kv.shape[2]
    rows = requests * max_nodes
    scores = rows * GROUP * (cache + max_nodes)
    table = pl.BlockSpec((1, max_nodes, HEAD), lambda r, *_: (r, 0, 0))
    return pl.pallas_call(
        heads_kernel,
        out_shape=jax.ShapeDtypeStruct((rows, GROUP * HEAD), jnp.bfloat16),
        grid_spec=pltpu.PrefetchScalarGridSpec(
            num_scalar_prefetch=2,
            grid=(requests,),
            in_specs=[pl.BlockSpec((max_nodes, part.shape[1]), lambda r, *_: (r, 0)) for part in parts]
            + [
                pl.BlockSpec(bias.shape, lambda r, *_: (0, 0)),
                pl.BlockSpec((1, max_nodes, max_nodes), lambda r, *_: (r, 0, 0)),
                table,
                table,
                pl.BlockSpec((1, 2, cache, HEAD), lambda r, *_: (r, 0, 0, 0)),
            ],
            out_specs=pl.BlockSpec((max_nodes, GROUP * HEAD), lambda r, *_: (r, 0)),
        ),
        compiler_params=pltpu.CompilerParams(vmem_limit_bytes=HEADS_LIMIT * 2**20),
        cost_estimate=pl.CostEstimate(flops=4 * scores * HEAD, bytes_accessed=4 * scores, transcendentals=scores),
    )(kept_counts, cache_len, *parts, bias, *tables, cache_kv)


Z = 4
CHIPS = 2 * Z
SPLIT = 3 * HEAD
NORM_LIMIT = DOT_LIMIT = HEADS_LIMIT = 60

GATE = ("a", ("own", "x0", "z1", "x1", "yx0", "yz1"))
MIDDLE = ("a", ("z2", "z3", "x3", "yz3", "yx1"))
LAST = ("a", ("yz2", "yx3", "x2", "yx2"))
PLAN = (
    "a + z0 z1", "a x z0 x0", "a x z1 x1", "a y z1 yz1", "a - w0 z3", "a + z1 z2", "a x z3 x3", "a y x0 yx0",
    "b + z0 z1", "b x z0 x0", "a y z3 yz3", GATE, "b - w0 z3", "b x z1 x1", "a y x1 yx1", "b + z1 z2", "b x z3 x3",
    "a y z2 yz2", "a x z2 x2", "a y x3 yx3", "b x z2 x2", "a y x2 yx2",
    MIDDLE, LAST, ("b", ("own", "z1", "x0", "z3", "x1", "z2", "x3", "x2")),
)
WAITED = {GATE: ("z1", "x0"), LAST: ("z1", "x0", "x1", "z3", "z2", "x3", "x2")}


def move(array, way):
    if way == "y":
        return lax.ppermute(array, "groups", [(0, 1), (1, 0)])
    if way == "x":
        pairs = [(i, i ^ 2) for i in range(4 * Z)]
    elif way == "core":
        pairs = [(i, i ^ 1) for i in range(4 * Z)]
    else:
        turn = 4 if way == "+" else -4
        pairs = [(i, (i + turn) % (4 * Z)) for i in range(4 * Z)]
    return lax.ppermute(array, "dp", pairs)


def ring(node_rows, kept_counts, parents, cache_len, cache_kv, norm_gain, w_qkv, b_qkv):
    depth = w_qkv.shape[0]
    group = lax.axis_index("groups")
    index = lax.axis_index("dp")
    z, x, core = index // 4, (index // 2) % 2, index % 2
    half = lax.dynamic_slice(w_qkv, (group * (depth // 2), SPLIT), (depth // 2, w_qkv.shape[1] - SPLIT))
    first = w_qkv[:, :SPLIT]
    tables = tree_tables(parents, cache_len)
    normed, copy = normalize_both(node_rows, move(node_rows, "core"), norm_gain, core, half, tables)
    pieces = {("a", "own"): w_qkv[:, SPLIT:], ("a", "z0"): half, ("a", "w0"): copy, ("b", "own"): first, ("b", "z0"): first}

    def place(name, chunk):
        if name == "own":
            return 2 * z + x
        side = 1 - group if name[0] == "y" else group
        chip = 2 * ((z - int(name[-1])) % Z) + (1 - x if "x" in name else x)
        return 2 * chip + side if chunk == "a" else chip

    sums = {"a": None, "b": None}
    for line in PLAN:
        if isinstance(line, tuple):
            chunk, names = line
            batch = [(pieces[chunk, name], place(name, chunk)) for name in names]
            copied = first if line == GATE else None
            unread = [pieces["b", name] for name in WAITED.get(line, ())]
            own_sum, other_sum, *copied = accumulate(normed, batch, sums[chunk], copied, unread)
            sums[chunk] = own_sum, other_sum
            if copied:
                pieces["b", "w0"] = copied[0]
        else:
            chunk, way, sent, received = line.split()
            pieces[chunk, received] = move(pieces[chunk, sent], way)

    parts = [part for chunk in "ba" for part in (sums[chunk][0], move(sums[chunk][1], "core"))]
    return attend_sums(parts, b_qkv.reshape(1, -1), tables, kept_counts, cache_len, cache_kv)


def on_device(node_rows, kept_counts, parents, cache_len, cache_kv, norm_gain, w_qkv, b_qkv):
    devices = lax.axis_size("dp")
    if devices == 4 * Z and w_qkv.shape[0] % 512 == 0:
        return ring(node_rows, kept_counts, parents, cache_len, cache_kv, norm_gain, w_qkv, b_qkv)
    weights = lax.all_gather(w_qkv, "dp", axis=0, tiled=True)
    normed = normalize(node_rows, norm_gain)
    tables = tree_tables(parents, cache_len)
    normed, weights, tables = lax.optimization_barrier((normed, weights, tables))
    projected = project(normed, weights, b_qkv)
    return attend(projected, *tables, kept_counts, cache_len, cache_kv)


def solution(mesh):
    return jax.shard_map(
        on_device,
        mesh=mesh,
        in_specs=(
            P(("groups", "dp"), None),
            P(("groups", "dp")),
            P(("groups", "dp"), None),
            P(("groups", "dp")),
            P(("groups", "dp"), None, None, None),
            P(),
            P("dp", None),
            P(),
        ),
        out_specs=P(("groups", "dp"), None),
        check_vma=False,
    )
```

```python
import functools
import math

import jax
import jax.numpy as jnp
from jax import lax
from jax.experimental import pallas as pl
from jax.experimental.pallas import tpu as pltpu
from jax.sharding import PartitionSpec as P

HEAD = 128
GROUP = 8
EPSILON = 1e-06
ROPE_BASE = 1000000.0
SCORE_SCALE = HEAD ** (-0.5) * math.log2(math.e)
HEADS_PER_STEP = 2


def normalize(row_block, norm_gain):
    values32 = row_block.astype(jnp.float32)
    mean_square = jnp.mean(values32 * values32, axis=-1, keepdims=True)
    return (values32 * lax.rsqrt(mean_square + EPSILON) * norm_gain).astype(jnp.bfloat16)


def tree_tables(parents, cache_len):
    max_nodes = parents.shape[1]
    positions = jnp.arange(max_nodes, dtype=jnp.int32)
    parent_link = (parents[:, :, None] == positions) & (positions[:, None] >= 1)
    reached = (parent_link | (positions[:, None] == positions)).astype(jnp.bfloat16)
    for squaring in range((max_nodes - 1).bit_length()):
        product = jnp.einsum("rij,rjk->rik", reached, reached, preferred_element_type=jnp.float32)
        reached = jnp.minimum(product, 1.0).astype(jnp.bfloat16)
    depth_of = jnp.sum(reached.astype(jnp.float32), axis=2) - 1.0
    placed = cache_len.astype(jnp.float32)[:, None] + depth_of
    frequency = ROPE_BASE ** (-(jnp.arange(HEAD // 2, dtype=jnp.float32) * 2.0 / HEAD))
    angles = placed[:, :, None] * frequency
    cosine = jnp.cos(angles)
    sine_part = jnp.sin(angles)
    tree_bias = jnp.where(reached > 0, 0.0, -jnp.inf).astype(jnp.float32)
    return (
        tree_bias,
        jnp.concatenate([cosine, cosine], axis=-1),
        jnp.concatenate([-sine_part, sine_part], axis=-1),
    )


def project_kernel(x_ref, w_ref, b_ref, o_ref, acc_ref):
    step = pl.program_id(0)
    part = jnp.dot(x_ref[...], w_ref[...], preferred_element_type=jnp.float32)

    @pl.when(step == 0)
    def _():
        acc_ref[...] = part

    @pl.when(step > 0)
    def _():
        acc_ref[...] += part

    @pl.when(step == pl.num_programs(0) - 1)
    def _():
        o_ref[...] = (acc_ref[...] + b_ref[...]).astype(o_ref.dtype)


def project(normed, weights, bias):
    rows, depth = normed.shape
    columns = weights.shape[1]
    tile = 1024
    return pl.pallas_call(
        project_kernel,
        out_shape=jax.ShapeDtypeStruct((rows, columns), jnp.bfloat16),
        grid=(depth // tile,),
        in_specs=[
            pl.BlockSpec((rows, tile), lambda k: (0, k)),
            pl.BlockSpec((tile, columns), lambda k: (k, 0)),
            pl.BlockSpec((1, columns), lambda k: (0, 0)),
        ],
        out_specs=pl.BlockSpec((rows, columns), lambda k: (0, 0)),
        scratch_shapes=[pltpu.VMEM((rows, columns), jnp.float32)],
        compiler_params=pltpu.CompilerParams(vmem_limit_bytes=60 * 2**20),
        cost_estimate=pl.CostEstimate(
            flops=2 * rows * depth * columns,
            bytes_accessed=2 * (rows * depth + depth * columns + rows * columns),
            transcendentals=0,
        ),
    )(normed, weights, bias.reshape(1, columns))


def rotate(vectors, cosine, sine_part):
    return (vectors * cosine + pltpu.roll(vectors, HEAD // 2, 1) * sine_part).astype(jnp.bfloat16)


def attend_kernel(kept_ref, len_ref, q_ref, kv_ref, bias_ref, cos_ref, sin_ref, cache_ref, o_ref, key_ref):
    request = pl.program_id(0)
    cosine = cos_ref[0]
    sine_part = sin_ref[0]

    @pl.when(pl.program_id(1) == 0)
    def _():
        key_ref[...] = rotate(kv_ref[:, :HEAD].astype(jnp.float32), cosine, sine_part)

    max_nodes = q_ref.shape[0]
    cache = cache_ref.shape[2]
    past = lax.broadcasted_iota(jnp.int32, (1, cache), 1) < len_ref[request]
    past_bias = jnp.where(past, 0.0, -jnp.inf)
    living = lax.broadcasted_iota(jnp.int32, (max_nodes, 1), 0) < kept_ref[request]
    transposed = (((1,), (1,)), ((), ()))
    for head in range(q_ref.shape[1] // HEAD):
        columns = slice(head * HEAD, (head + 1) * HEAD)
        query = rotate(q_ref[:, columns].astype(jnp.float32), cosine, sine_part)
        past_scores = lax.dot_general(query, cache_ref[0, 0], transposed, preferred_element_type=jnp.float32)
        past_scores = past_scores * SCORE_SCALE + past_bias
        tree_scores = lax.dot_general(query, key_ref[...], transposed, preferred_element_type=jnp.float32)
        tree_scores = tree_scores * SCORE_SCALE + bias_ref[0]
        top = jnp.maximum(
            jnp.max(past_scores, axis=1, keepdims=True), jnp.max(tree_scores, axis=1, keepdims=True)
        )
        past_weights = jnp.exp2(past_scores - top)
        tree_weights = jnp.exp2(tree_scores - top)
        total = jnp.sum(past_weights, axis=1, keepdims=True) + jnp.sum(tree_weights, axis=1, keepdims=True)
        inverse = 1.0 / total
        blended = jnp.dot(
            (past_weights * inverse).astype(jnp.bfloat16), cache_ref[0, 1], preferred_element_type=jnp.float32
        )
        blended += jnp.dot(
            (tree_weights * inverse).astype(jnp.bfloat16), kv_ref[:, HEAD:], preferred_element_type=jnp.float32
        )
        o_ref[:, columns] = jnp.where(living, blended, 0.0).astype(o_ref.dtype)


def attend(projected, tree_bias, cosine, sine_part, kept_counts, cache_len, cache_kv):
    requests, max_nodes = tree_bias.shape[:2]
    cache = cache_kv.shape[2]
    width = HEADS_PER_STEP * HEAD
    table = pl.BlockSpec((1, max_nodes, HEAD), lambda r, h, *_: (r, 0, 0))
    return pl.pallas_call(
        attend_kernel,
        out_shape=jax.ShapeDtypeStruct((requests * max_nodes, GROUP * HEAD), jnp.bfloat16),
        grid_spec=pltpu.PrefetchScalarGridSpec(
            num_scalar_prefetch=2,
            grid=(requests, GROUP // HEADS_PER_STEP),
            in_specs=[
                pl.BlockSpec((max_nodes, width), lambda r, h, *_: (r, h)),
                pl.BlockSpec((max_nodes, 2 * HEAD), lambda r, h, *_: (r, GROUP // 2)),
                pl.BlockSpec((1, max_nodes, max_nodes), lambda r, h, *_: (r, 0, 0)),
                table,
                table,
                pl.BlockSpec((1, 2, cache, HEAD), lambda r, h, *_: (r, 0, 0, 0)),
            ],
            out_specs=pl.BlockSpec((max_nodes, width), lambda r, h, *_: (r, h)),
            scratch_shapes=[pltpu.VMEM((max_nodes, HEAD), jnp.bfloat16)],
        ),
        compiler_params=pltpu.CompilerParams(vmem_limit_bytes=60 * 2**20),
    )(kept_counts, cache_len, projected, projected, tree_bias, cosine, sine_part, cache_kv)


def norm_kernel(steps, core_ref, x_ref, other_ref, gain_ref, w_ref, *refs):
    out_ref, copy_ref = refs[-2:]
    copy_ref[...] = w_ref[...]

    def work(rows_ref):
        values32 = rows_ref[...].astype(jnp.float32)
        mean_square = jnp.mean(values32 * values32, axis=-1, keepdims=True)
        factor = lax.rsqrt(mean_square + EPSILON)
        width = rows_ref.shape[1] // (2 * CHIPS)
        for chip in range(CHIPS):
            source = pl.ds(pl.multiple_of((2 * chip + core_ref[0]) * width, width), width)
            block = rows_ref[:, source].astype(jnp.float32) * factor * gain_ref[:, source]
            out_ref[:, chip * width : (chip + 1) * width] = block.astype(jnp.bfloat16)

    pl.when(pl.program_id(0) < steps)(lambda: work(x_ref))
    pl.when(pl.program_id(0) >= steps)(lambda: work(other_ref))


def normalize_both(own_rows, other_rows, norm_gain, core, columns, unread):
    rows, depth = own_rows.shape
    tile = 128
    steps = rows // tile
    copy_spec = pl.BlockSpec((columns.shape[0] // (2 * steps), columns.shape[1]), lambda r, *_: (r, 0))
    return pl.pallas_call(
        functools.partial(norm_kernel, steps),
        out_shape=(
            jax.ShapeDtypeStruct((2 * rows, depth // 2), jnp.bfloat16),
            jax.ShapeDtypeStruct(columns.shape, columns.dtype),
        ),
        grid_spec=pltpu.PrefetchScalarGridSpec(
            num_scalar_prefetch=1,
            grid=(2 * steps,),
            in_specs=[
                pl.BlockSpec((tile, depth), lambda r, *_: (jnp.minimum(r, steps - 1), 0)),
                pl.BlockSpec((tile, depth), lambda r, *_: (jnp.maximum(r - steps, 0), 0)),
                pl.BlockSpec((1, depth), lambda r, *_: (0, 0)),
                copy_spec,
                *[pl.BlockSpec(memory_space=pl.ANY)] * len(unread),
            ],
            out_specs=(pl.BlockSpec((tile, depth // 2), lambda r, *_: (r, 0)), copy_spec),
        ),
        compiler_params=pltpu.CompilerParams(vmem_limit_bytes=NORM_LIMIT * 2**20),
        cost_estimate=pl.CostEstimate(flops=8 * rows * depth, bytes_accessed=6 * rows * depth, transcendentals=0),
    )(core.reshape(1), own_rows, other_rows, norm_gain.reshape(1, depth), columns, *unread)


def accumulate_kernel(count, unread, first, steps, copies, place_ref, *refs):
    refs = refs[: 2 * count] + refs[2 * count + unread :]
    if copies:
        refs[-1][...] = refs[2 * count][...]
        refs = refs[: 2 * count] + refs[2 * count + 1 : -1]
    x_refs, piece_refs, rest = refs[:count], refs[count : 2 * count], refs[2 * count :]

    def side(which):
        total = None if first else rest[which][...]
        for x_ref, w_ref in zip(x_refs, piece_refs):
            part = jnp.dot(x_ref[...], w_ref[...], preferred_element_type=jnp.float32)
            total = part if total is None else total + part
        rest[which if first else 2 + which][...] = total

    pl.when(pl.program_id(0) < steps)(lambda: side(1))
    pl.when(pl.program_id(0) >= steps)(lambda: side(0))


def accumulate(normed, pieces, sums, copied=None, unread=()):
    rows = normed.shape[0] // 2
    columns = pieces[0][0].shape[1]
    tile = 256
    steps = rows // tile
    count = len(pieces)
    depth = sum(array.shape[0] for array, _ in pieces)
    places = jnp.stack([place for _, place in pieces]).astype(jnp.int32)

    def rows_spec(index):
        return pl.BlockSpec(
            (tile, pieces[index][0].shape[0]), lambda r, place_ref: (lax.rem(r + steps, 2 * steps), place_ref[index])
        )

    sum_specs = (
        pl.BlockSpec((tile, columns), lambda r, *_: (jnp.maximum(r - steps, 0), 0)),
        pl.BlockSpec((tile, columns), lambda r, *_: (jnp.minimum(r, steps - 1), 0)),
    )
    out = jax.ShapeDtypeStruct((rows, columns), jnp.float32)
    first = sums is None
    extra = [] if copied is None else [copied]
    copy_specs = [pl.BlockSpec((array.shape[0] // (2 * steps), array.shape[1]), lambda r, *_: (r, 0)) for array in extra]
    return pl.pallas_call(
        functools.partial(accumulate_kernel, count, len(unread), first, steps, bool(extra)),
        out_shape=(out, out, *[jax.ShapeDtypeStruct(array.shape, array.dtype) for array in extra]),
        grid_spec=pltpu.PrefetchScalarGridSpec(
            num_scalar_prefetch=1,
            grid=(2 * steps,),
            in_specs=[rows_spec(i) for i in range(count)]
            + [pl.BlockSpec(array.shape, lambda r, *_: (0, 0)) for array, _ in pieces]
            + [pl.BlockSpec(memory_space=pl.ANY)] * len(unread)
            + copy_specs
            + ([] if first else list(sum_specs)),
            out_specs=(*sum_specs, *copy_specs),
        ),
        input_output_aliases={} if first else {1 + 2 * count + len(unread) + len(extra) + i: i for i in range(2)},
        compiler_params=pltpu.CompilerParams(vmem_limit_bytes=DOT_LIMIT * 2**20),
        cost_estimate=pl.CostEstimate(
            flops=4 * rows * depth * columns,
            bytes_accessed=4 * rows * depth + 2 * depth * columns + (8 if first else 16) * rows * columns,
            transcendentals=0,
        ),
    )(places, *([normed] * count), *[array for array, _ in pieces], *unread, *extra, *(() if first else sums))


def softmax_values(query, past_keys, past_values, past_bias, node_keys, node_values, tree_bias, living):
    transposed = (((1,), (1,)), ((), ()))
    past_scores = lax.dot_general(query, past_keys, transposed, preferred_element_type=jnp.float32)
    past_scores = past_scores * SCORE_SCALE + past_bias
    tree_scores = lax.dot_general(query, node_keys, transposed, preferred_element_type=jnp.float32)
    tree_scores = tree_scores * SCORE_SCALE + tree_bias
    top = jnp.maximum(jnp.max(past_scores, axis=1, keepdims=True), jnp.max(tree_scores, axis=1, keepdims=True))
    past_weights = jnp.exp2(past_scores - top)
    tree_weights = jnp.exp2(tree_scores - top)
    total = jnp.sum(past_weights, axis=1, keepdims=True) + jnp.sum(tree_weights, axis=1, keepdims=True)
    inverse = 1.0 / total
    blended = jnp.dot((past_weights * inverse).astype(jnp.bfloat16), past_values, preferred_element_type=jnp.float32)
    blended += jnp.dot((tree_weights * inverse).astype(jnp.bfloat16), node_values, preferred_element_type=jnp.float32)
    return jnp.where(living, blended, 0.0).astype(jnp.bfloat16)


def masks(kept_ref, len_ref, request, max_nodes, cache):
    past = lax.broadcasted_iota(jnp.int32, (1, cache), 1) < len_ref[request]
    living = lax.broadcasted_iota(jnp.int32, (max_nodes, 1), 0) < kept_ref[request]
    return jnp.where(past, 0.0, -jnp.inf), living


def heads_kernel(kept_ref, len_ref, own_b, got_b, own_a, got_a, b_ref, bias_ref, cos_ref, sin_ref, cache_ref, o_ref):
    past_bias, living = masks(kept_ref, len_ref, pl.program_id(0), own_a.shape[0], cache_ref.shape[2])
    cosine, sine_part = cos_ref[0], sin_ref[0]

    def column_block(index):
        own_ref, got_ref, start = (own_b, got_b, 0) if index * HEAD < SPLIT else (own_a, got_a, SPLIT)
        columns = slice(index * HEAD - start, (index + 1) * HEAD - start)
        bias = b_ref[:, index * HEAD : (index + 1) * HEAD]
        return (own_ref[:, columns] + got_ref[:, columns] + bias).astype(jnp.bfloat16)

    node_keys = rotate(column_block(GROUP).astype(jnp.float32), cosine, sine_part)
    node_values = column_block(GROUP + 1)
    for head in reversed(range(GROUP)):
        query = rotate(column_block(head).astype(jnp.float32), cosine, sine_part)
        o_ref[:, head * HEAD : (head + 1) * HEAD] = softmax_values(
            query, cache_ref[0, 0], cache_ref[0, 1], past_bias, node_keys, node_values, bias_ref[0], living
        )


def attend_sums(parts, bias, tables, kept_counts, cache_len, cache_kv):
    requests, max_nodes = tables[0].shape[:2]
    cache = cache_kv.shape[2]
    rows = requests * max_nodes
    scores = rows * GROUP * (cache + max_nodes)
    table = pl.BlockSpec((1, max_nodes, HEAD), lambda r, *_: (r, 0, 0))
    return pl.pallas_call(
        heads_kernel,
        out_shape=jax.ShapeDtypeStruct((rows, GROUP * HEAD), jnp.bfloat16),
        grid_spec=pltpu.PrefetchScalarGridSpec(
            num_scalar_prefetch=2,
            grid=(requests,),
            in_specs=[pl.BlockSpec((max_nodes, part.shape[1]), lambda r, *_: (r, 0)) for part in parts]
            + [
                pl.BlockSpec(bias.shape, lambda r, *_: (0, 0)),
                pl.BlockSpec((1, max_nodes, max_nodes), lambda r, *_: (r, 0, 0)),
                table,
                table,
                pl.BlockSpec((1, 2, cache, HEAD), lambda r, *_: (r, 0, 0, 0)),
            ],
            out_specs=pl.BlockSpec((max_nodes, GROUP * HEAD), lambda r, *_: (r, 0)),
        ),
        compiler_params=pltpu.CompilerParams(vmem_limit_bytes=HEADS_LIMIT * 2**20),
        cost_estimate=pl.CostEstimate(flops=4 * scores * HEAD, bytes_accessed=4 * scores, transcendentals=scores),
    )(kept_counts, cache_len, *parts, bias, *tables, cache_kv)


Z = 4
CHIPS = 2 * Z
SPLIT = 3 * HEAD
NORM_LIMIT = DOT_LIMIT = 60
HEADS_LIMIT = 30

GATE = ("a", ("own", "x0", "z1", "x1", "yx0", "yz1", "z3"))
MIDDLE = ("a", ("z2", "x3", "yz3", "yx1"))
LAST = ("a", ("yz2", "yx3", "x2", "yx2"))
PLAN = (
    "a + z0 z1", "a x z0 x0", "a x z1 x1", "a y z1 yz1", "a - z0 z3", "a + z1 z2", "a x z3 x3", "a y x0 yx0",
    "b + z0 z1", "b x z0 x0", "a y z3 yz3", GATE, "b - w0 z3", "b x z1 x1", "a y x1 yx1", "b + z1 z2", "b x z3 x3",
    "a y z2 yz2", "a x z2 x2", "a y x3 yx3", "b x z2 x2", "a y x2 yx2",
    MIDDLE, LAST, ("b", ("own", "z1", "x0", "z3", "x1", "z2", "x3", "x2")),
)
WAITED = {GATE: ("z1", "x0"), LAST: ("z1", "x0", "x1", "z3", "z2", "x3", "x2")}


def move(array, way):
    if way == "y":
        return lax.ppermute(array, "groups", [(0, 1), (1, 0)])
    if way == "x":
        pairs = [(i, i ^ 2) for i in range(4 * Z)]
    elif way == "core":
        pairs = [(i, i ^ 1) for i in range(4 * Z)]
    else:
        turn = 4 if way == "+" else -4
        pairs = [(i, (i + turn) % (4 * Z)) for i in range(4 * Z)]
    return lax.ppermute(array, "dp", pairs)


def ring(node_rows, kept_counts, parents, cache_len, cache_kv, norm_gain, w_qkv, b_qkv):
    depth = w_qkv.shape[0]
    group = lax.axis_index("groups")
    index = lax.axis_index("dp")
    z, x, core = index // 4, (index // 2) % 2, index % 2
    half = lax.dynamic_slice(w_qkv, (group * (depth // 2), SPLIT), (depth // 2, w_qkv.shape[1] - SPLIT))
    first = w_qkv[:, :SPLIT]
    tables = tree_tables(parents, cache_len)
    normed, copy = normalize_both(node_rows, move(node_rows, "core"), norm_gain, core, first, tables)
    pieces = {("a", "own"): w_qkv[:, SPLIT:], ("a", "z0"): half, ("b", "own"): first, ("b", "z0"): copy}

    def place(name, chunk):
        if name == "own":
            return 2 * z + x
        side = 1 - group if name[0] == "y" else group
        chip = 2 * ((z - int(name[-1])) % Z) + (1 - x if "x" in name else x)
        return 2 * chip + side if chunk == "a" else chip

    sums = {"a": None, "b": None}
    for line in PLAN:
        if isinstance(line, tuple):
            chunk, names = line
            batch = [(pieces[chunk, name], place(name, chunk)) for name in names]
            copied = first if line == GATE else None
            unread = [pieces["b", name] for name in WAITED.get(line, ())]
            own_sum, other_sum, *copied = accumulate(normed, batch, sums[chunk], copied, unread)
            sums[chunk] = own_sum, other_sum
            if copied:
                pieces["b", "w0"] = copied[0]
        else:
            chunk, way, sent, received = line.split()
            pieces[chunk, received] = move(pieces[chunk, sent], way)

    parts = [part for chunk in "ba" for part in (sums[chunk][0], move(sums[chunk][1], "core"))]
    return attend_sums(parts, b_qkv.reshape(1, -1), tables, kept_counts, cache_len, cache_kv)


def on_device(node_rows, kept_counts, parents, cache_len, cache_kv, norm_gain, w_qkv, b_qkv):
    devices = lax.axis_size("dp")
    if devices == 4 * Z and w_qkv.shape[0] % 512 == 0:
        return ring(node_rows, kept_counts, parents, cache_len, cache_kv, norm_gain, w_qkv, b_qkv)
    weights = lax.all_gather(w_qkv, "dp", axis=0, tiled=True)
    normed = normalize(node_rows, norm_gain)
    tables = tree_tables(parents, cache_len)
    normed, weights, tables = lax.optimization_barrier((normed, weights, tables))
    projected = project(normed, weights, b_qkv)
    return attend(projected, *tables, kept_counts, cache_len, cache_kv)


def solution(mesh):
    return jax.shard_map(
        on_device,
        mesh=mesh,
        in_specs=(
            P(("groups", "dp"), None),
            P(("groups", "dp")),
            P(("groups", "dp"), None),
            P(("groups", "dp")),
            P(("groups", "dp"), None, None, None),
            P(),
            P("dp", None),
            P(),
        ),
        out_specs=P(("groups", "dp"), None),
        check_vma=False,
    )
```

```python
import functools
import math

import jax
import jax.numpy as jnp
from jax import lax
from jax.experimental import pallas as pl
from jax.experimental.pallas import tpu as pltpu
from jax.sharding import PartitionSpec as P

HEAD = 128
GROUP = 8
EPSILON = 1e-06
ROPE_BASE = 1000000.0
SCORE_SCALE = HEAD ** (-0.5) * math.log2(math.e)
HEADS_PER_STEP = 2


def normalize(row_block, norm_gain):
    values32 = row_block.astype(jnp.float32)
    mean_square = jnp.mean(values32 * values32, axis=-1, keepdims=True)
    return (values32 * lax.rsqrt(mean_square + EPSILON) * norm_gain).astype(jnp.bfloat16)


def tree_tables(parents, cache_len):
    max_nodes = parents.shape[1]
    positions = jnp.arange(max_nodes, dtype=jnp.int32)
    parent_link = (parents[:, :, None] == positions) & (positions[:, None] >= 1)
    reached = (parent_link | (positions[:, None] == positions)).astype(jnp.bfloat16)
    for squaring in range((max_nodes - 1).bit_length()):
        product = jnp.einsum("rij,rjk->rik", reached, reached, preferred_element_type=jnp.float32)
        reached = jnp.minimum(product, 1.0).astype(jnp.bfloat16)
    depth_of = jnp.sum(reached.astype(jnp.float32), axis=2) - 1.0
    placed = cache_len.astype(jnp.float32)[:, None] + depth_of
    frequency = ROPE_BASE ** (-(jnp.arange(HEAD // 2, dtype=jnp.float32) * 2.0 / HEAD))
    angles = placed[:, :, None] * frequency
    cosine = jnp.cos(angles)
    sine_part = jnp.sin(angles)
    tree_bias = jnp.where(reached > 0, 0.0, -jnp.inf).astype(jnp.float32)
    return (
        tree_bias,
        jnp.concatenate([cosine, cosine], axis=-1),
        jnp.concatenate([-sine_part, sine_part], axis=-1),
    )


def project_kernel(x_ref, w_ref, b_ref, o_ref, acc_ref):
    step = pl.program_id(0)
    part = jnp.dot(x_ref[...], w_ref[...], preferred_element_type=jnp.float32)

    @pl.when(step == 0)
    def _():
        acc_ref[...] = part

    @pl.when(step > 0)
    def _():
        acc_ref[...] += part

    @pl.when(step == pl.num_programs(0) - 1)
    def _():
        o_ref[...] = (acc_ref[...] + b_ref[...]).astype(o_ref.dtype)


def project(normed, weights, bias):
    rows, depth = normed.shape
    columns = weights.shape[1]
    tile = 1024
    return pl.pallas_call(
        project_kernel,
        out_shape=jax.ShapeDtypeStruct((rows, columns), jnp.bfloat16),
        grid=(depth // tile,),
        in_specs=[
            pl.BlockSpec((rows, tile), lambda k: (0, k)),
            pl.BlockSpec((tile, columns), lambda k: (k, 0)),
            pl.BlockSpec((1, columns), lambda k: (0, 0)),
        ],
        out_specs=pl.BlockSpec((rows, columns), lambda k: (0, 0)),
        scratch_shapes=[pltpu.VMEM((rows, columns), jnp.float32)],
        compiler_params=pltpu.CompilerParams(vmem_limit_bytes=60 * 2**20),
        cost_estimate=pl.CostEstimate(
            flops=2 * rows * depth * columns,
            bytes_accessed=2 * (rows * depth + depth * columns + rows * columns),
            transcendentals=0,
        ),
    )(normed, weights, bias.reshape(1, columns))


def rotate(vectors, cosine, sine_part):
    return (vectors * cosine + pltpu.roll(vectors, HEAD // 2, 1) * sine_part).astype(jnp.bfloat16)


def attend_kernel(kept_ref, len_ref, q_ref, kv_ref, bias_ref, cos_ref, sin_ref, cache_ref, o_ref, key_ref):
    request = pl.program_id(0)
    cosine = cos_ref[0]
    sine_part = sin_ref[0]

    @pl.when(pl.program_id(1) == 0)
    def _():
        key_ref[...] = rotate(kv_ref[:, :HEAD].astype(jnp.float32), cosine, sine_part)

    max_nodes = q_ref.shape[0]
    cache = cache_ref.shape[2]
    past = lax.broadcasted_iota(jnp.int32, (1, cache), 1) < len_ref[request]
    past_bias = jnp.where(past, 0.0, -jnp.inf)
    living = lax.broadcasted_iota(jnp.int32, (max_nodes, 1), 0) < kept_ref[request]
    transposed = (((1,), (1,)), ((), ()))
    for head in range(q_ref.shape[1] // HEAD):
        columns = slice(head * HEAD, (head + 1) * HEAD)
        query = rotate(q_ref[:, columns].astype(jnp.float32), cosine, sine_part)
        past_scores = lax.dot_general(query, cache_ref[0, 0], transposed, preferred_element_type=jnp.float32)
        past_scores = past_scores * SCORE_SCALE + past_bias
        tree_scores = lax.dot_general(query, key_ref[...], transposed, preferred_element_type=jnp.float32)
        tree_scores = tree_scores * SCORE_SCALE + bias_ref[0]
        top = jnp.maximum(
            jnp.max(past_scores, axis=1, keepdims=True), jnp.max(tree_scores, axis=1, keepdims=True)
        )
        past_weights = jnp.exp2(past_scores - top)
        tree_weights = jnp.exp2(tree_scores - top)
        total = jnp.sum(past_weights, axis=1, keepdims=True) + jnp.sum(tree_weights, axis=1, keepdims=True)
        inverse = 1.0 / total
        blended = jnp.dot(
            (past_weights * inverse).astype(jnp.bfloat16), cache_ref[0, 1], preferred_element_type=jnp.float32
        )
        blended += jnp.dot(
            (tree_weights * inverse).astype(jnp.bfloat16), kv_ref[:, HEAD:], preferred_element_type=jnp.float32
        )
        o_ref[:, columns] = jnp.where(living, blended, 0.0).astype(o_ref.dtype)


def attend(projected, tree_bias, cosine, sine_part, kept_counts, cache_len, cache_kv):
    requests, max_nodes = tree_bias.shape[:2]
    cache = cache_kv.shape[2]
    width = HEADS_PER_STEP * HEAD
    table = pl.BlockSpec((1, max_nodes, HEAD), lambda r, h, *_: (r, 0, 0))
    return pl.pallas_call(
        attend_kernel,
        out_shape=jax.ShapeDtypeStruct((requests * max_nodes, GROUP * HEAD), jnp.bfloat16),
        grid_spec=pltpu.PrefetchScalarGridSpec(
            num_scalar_prefetch=2,
            grid=(requests, GROUP // HEADS_PER_STEP),
            in_specs=[
                pl.BlockSpec((max_nodes, width), lambda r, h, *_: (r, h)),
                pl.BlockSpec((max_nodes, 2 * HEAD), lambda r, h, *_: (r, GROUP // 2)),
                pl.BlockSpec((1, max_nodes, max_nodes), lambda r, h, *_: (r, 0, 0)),
                table,
                table,
                pl.BlockSpec((1, 2, cache, HEAD), lambda r, h, *_: (r, 0, 0, 0)),
            ],
            out_specs=pl.BlockSpec((max_nodes, width), lambda r, h, *_: (r, h)),
            scratch_shapes=[pltpu.VMEM((max_nodes, HEAD), jnp.bfloat16)],
        ),
        compiler_params=pltpu.CompilerParams(vmem_limit_bytes=60 * 2**20),
    )(kept_counts, cache_len, projected, projected, tree_bias, cosine, sine_part, cache_kv)


def norm_kernel(steps, core_ref, x_ref, other_ref, gain_ref, w_ref, *refs):
    out_ref, copy_ref = refs[-2:]
    copy_ref[...] = w_ref[...]

    def work(rows_ref):
        values32 = rows_ref[...].astype(jnp.float32)
        mean_square = jnp.mean(values32 * values32, axis=-1, keepdims=True)
        factor = lax.rsqrt(mean_square + EPSILON)
        width = rows_ref.shape[1] // (2 * CHIPS)
        for chip in range(CHIPS):
            source = pl.ds(pl.multiple_of((2 * chip + core_ref[0]) * width, width), width)
            block = rows_ref[:, source].astype(jnp.float32) * factor * gain_ref[:, source]
            out_ref[:, chip * width : (chip + 1) * width] = block.astype(jnp.bfloat16)

    pl.when(pl.program_id(0) < steps)(lambda: work(x_ref))
    pl.when(pl.program_id(0) >= steps)(lambda: work(other_ref))


def normalize_both(own_rows, other_rows, norm_gain, core, columns, unread):
    rows, depth = own_rows.shape
    tile = 128
    steps = rows // tile
    copy_spec = pl.BlockSpec((columns.shape[0] // (2 * steps), columns.shape[1]), lambda r, *_: (r, 0))
    return pl.pallas_call(
        functools.partial(norm_kernel, steps),
        out_shape=(
            jax.ShapeDtypeStruct((2 * rows, depth // 2), jnp.bfloat16),
            jax.ShapeDtypeStruct(columns.shape, columns.dtype),
        ),
        grid_spec=pltpu.PrefetchScalarGridSpec(
            num_scalar_prefetch=1,
            grid=(2 * steps,),
            in_specs=[
                pl.BlockSpec((tile, depth), lambda r, *_: (jnp.minimum(r, steps - 1), 0)),
                pl.BlockSpec((tile, depth), lambda r, *_: (jnp.maximum(r - steps, 0), 0)),
                pl.BlockSpec((1, depth), lambda r, *_: (0, 0)),
                copy_spec,
                *[pl.BlockSpec(memory_space=pl.ANY)] * len(unread),
            ],
            out_specs=(pl.BlockSpec((tile, depth // 2), lambda r, *_: (r, 0)), copy_spec),
        ),
        compiler_params=pltpu.CompilerParams(vmem_limit_bytes=NORM_LIMIT * 2**20),
        cost_estimate=pl.CostEstimate(flops=8 * rows * depth, bytes_accessed=6 * rows * depth, transcendentals=0),
    )(core.reshape(1), own_rows, other_rows, norm_gain.reshape(1, depth), columns, *unread)


def accumulate_kernel(count, unread, first, steps, copies, place_ref, *refs):
    refs = refs[: 2 * count] + refs[2 * count + unread :]
    if copies:
        refs[-1][...] = refs[2 * count][...]
        refs = refs[: 2 * count] + refs[2 * count + 1 : -1]
    x_refs, piece_refs, rest = refs[:count], refs[count : 2 * count], refs[2 * count :]

    def side(which):
        total = None if first else rest[which][...]
        for x_ref, w_ref in zip(x_refs, piece_refs):
            part = jnp.dot(x_ref[...], w_ref[...], preferred_element_type=jnp.float32)
            total = part if total is None else total + part
        rest[which if first else 2 + which][...] = total

    pl.when(pl.program_id(0) < steps)(lambda: side(1))
    pl.when(pl.program_id(0) >= steps)(lambda: side(0))


def accumulate(normed, pieces, sums, copied=None, unread=()):
    rows = normed.shape[0] // 2
    columns = pieces[0][0].shape[1]
    tile = 256
    steps = rows // tile
    count = len(pieces)
    depth = sum(array.shape[0] for array, _ in pieces)
    places = jnp.stack([place for _, place in pieces]).astype(jnp.int32)

    def rows_spec(index):
        return pl.BlockSpec(
            (tile, pieces[index][0].shape[0]), lambda r, place_ref: (lax.rem(r + steps, 2 * steps), place_ref[index])
        )

    sum_specs = (
        pl.BlockSpec((tile, columns), lambda r, *_: (jnp.maximum(r - steps, 0), 0)),
        pl.BlockSpec((tile, columns), lambda r, *_: (jnp.minimum(r, steps - 1), 0)),
    )
    out = jax.ShapeDtypeStruct((rows, columns), jnp.float32)
    first = sums is None
    extra = [] if copied is None else [copied]
    copy_specs = [pl.BlockSpec((array.shape[0] // (2 * steps), array.shape[1]), lambda r, *_: (r, 0)) for array in extra]
    return pl.pallas_call(
        functools.partial(accumulate_kernel, count, len(unread), first, steps, bool(extra)),
        out_shape=(out, out, *[jax.ShapeDtypeStruct(array.shape, array.dtype) for array in extra]),
        grid_spec=pltpu.PrefetchScalarGridSpec(
            num_scalar_prefetch=1,
            grid=(2 * steps,),
            in_specs=[rows_spec(i) for i in range(count)]
            + [pl.BlockSpec(array.shape, lambda r, *_: (0, 0)) for array, _ in pieces]
            + [pl.BlockSpec(memory_space=pl.ANY)] * len(unread)
            + copy_specs
            + ([] if first else list(sum_specs)),
            out_specs=(*sum_specs, *copy_specs),
        ),
        input_output_aliases={} if first else {1 + 2 * count + len(unread) + len(extra) + i: i for i in range(2)},
        compiler_params=pltpu.CompilerParams(vmem_limit_bytes=DOT_LIMIT * 2**20),
        cost_estimate=pl.CostEstimate(
            flops=4 * rows * depth * columns,
            bytes_accessed=4 * rows * depth + 2 * depth * columns + (8 if first else 16) * rows * columns,
            transcendentals=0,
        ),
    )(places, *([normed] * count), *[array for array, _ in pieces], *unread, *extra, *(() if first else sums))


def softmax_values(query, past_keys, past_values, past_bias, node_keys, node_values, tree_bias, living):
    transposed = (((1,), (1,)), ((), ()))
    past_scores = lax.dot_general(query, past_keys, transposed, preferred_element_type=jnp.float32)
    past_scores = past_scores * SCORE_SCALE + past_bias
    tree_scores = lax.dot_general(query, node_keys, transposed, preferred_element_type=jnp.float32)
    tree_scores = tree_scores * SCORE_SCALE + tree_bias
    top = jnp.maximum(jnp.max(past_scores, axis=1, keepdims=True), jnp.max(tree_scores, axis=1, keepdims=True))
    past_weights = jnp.exp2(past_scores - top)
    tree_weights = jnp.exp2(tree_scores - top)
    total = jnp.sum(past_weights, axis=1, keepdims=True) + jnp.sum(tree_weights, axis=1, keepdims=True)
    inverse = 1.0 / total
    blended = jnp.dot((past_weights * inverse).astype(jnp.bfloat16), past_values, preferred_element_type=jnp.float32)
    blended += jnp.dot((tree_weights * inverse).astype(jnp.bfloat16), node_values, preferred_element_type=jnp.float32)
    return jnp.where(living, blended, 0.0).astype(jnp.bfloat16)


def masks(kept_ref, len_ref, request, max_nodes, cache):
    past = lax.broadcasted_iota(jnp.int32, (1, cache), 1) < len_ref[request]
    living = lax.broadcasted_iota(jnp.int32, (max_nodes, 1), 0) < kept_ref[request]
    return jnp.where(past, 0.0, -jnp.inf), living


def heads_kernel(kept_ref, len_ref, own_b, got_b, own_a, got_a, b_ref, bias_ref, cos_ref, sin_ref, cache_ref, o_ref):
    past_bias, living = masks(kept_ref, len_ref, pl.program_id(0), own_a.shape[0], cache_ref.shape[2])
    cosine, sine_part = cos_ref[0], sin_ref[0]

    def column_block(index):
        own_ref, got_ref, start = (own_b, got_b, 0) if index * HEAD < SPLIT else (own_a, got_a, SPLIT)
        columns = slice(index * HEAD - start, (index + 1) * HEAD - start)
        bias = b_ref[:, index * HEAD : (index + 1) * HEAD]
        return (own_ref[:, columns] + got_ref[:, columns] + bias).astype(jnp.bfloat16)

    node_keys = rotate(column_block(GROUP).astype(jnp.float32), cosine, sine_part)
    node_values = column_block(GROUP + 1)
    for head in reversed(range(GROUP)):
        query = rotate(column_block(head).astype(jnp.float32), cosine, sine_part)
        o_ref[:, head * HEAD : (head + 1) * HEAD] = softmax_values(
            query, cache_ref[0, 0], cache_ref[0, 1], past_bias, node_keys, node_values, bias_ref[0], living
        )


def attend_sums(parts, bias, tables, kept_counts, cache_len, cache_kv):
    requests, max_nodes = tables[0].shape[:2]
    cache = cache_kv.shape[2]
    rows = requests * max_nodes
    scores = rows * GROUP * (cache + max_nodes)
    table = pl.BlockSpec((1, max_nodes, HEAD), lambda r, *_: (r, 0, 0))
    return pl.pallas_call(
        heads_kernel,
        out_shape=jax.ShapeDtypeStruct((rows, GROUP * HEAD), jnp.bfloat16),
        grid_spec=pltpu.PrefetchScalarGridSpec(
            num_scalar_prefetch=2,
            grid=(requests,),
            in_specs=[pl.BlockSpec((max_nodes, part.shape[1]), lambda r, *_: (r, 0)) for part in parts]
            + [
                pl.BlockSpec(bias.shape, lambda r, *_: (0, 0)),
                pl.BlockSpec((1, max_nodes, max_nodes), lambda r, *_: (r, 0, 0)),
                table,
                table,
                pl.BlockSpec((1, 2, cache, HEAD), lambda r, *_: (r, 0, 0, 0)),
            ],
            out_specs=pl.BlockSpec((max_nodes, GROUP * HEAD), lambda r, *_: (r, 0)),
        ),
        compiler_params=pltpu.CompilerParams(vmem_limit_bytes=HEADS_LIMIT * 2**20),
        cost_estimate=pl.CostEstimate(flops=4 * scores * HEAD, bytes_accessed=4 * scores, transcendentals=scores),
    )(kept_counts, cache_len, *parts, bias, *tables, cache_kv)


Z = 4
CHIPS = 2 * Z
SPLIT = 3 * HEAD
NORM_LIMIT = DOT_LIMIT = 60
HEADS_LIMIT = 30

GATE = ("a", ("own", "x0", "z1", "x1", "yx0", "yz1", "z3"))
MIDDLE = ("a", ("z2", "x3", "yz3", "yx1"))
LAST = ("a", ("yz2", "yx3", "x2", "yx2"))
PLAN = (
    "a + z0 z1", "a x z0 x0", "a x z1 x1", "a y z1 yz1", "a - z0 z3", "a + z1 z2", "a x z3 x3", "a y x0 yx0",
    "b + z0 z1", "b x z0 x0", "a y z3 yz3", GATE, "b - w0 z3", "b x z1 x1", "a y x1 yx1", "b + z1 z2", "b x z3 x3",
    "a y z2 yz2", "a x z2 x2", "a y x3 yx3", "b x z2 x2", "a y x2 yx2",
    MIDDLE, LAST, ("b", ("own", "z1", "x0", "z3", "x1", "z2", "x3", "x2")),
)
WAITED = {GATE: ("z1", "x0"), MIDDLE: ("z3", "x1"), LAST: ("z1", "x0", "x1", "z3", "z2", "x3", "x2")}


def move(array, way):
    if way == "y":
        return lax.ppermute(array, "groups", [(0, 1), (1, 0)])
    if way == "x":
        pairs = [(i, i ^ 2) for i in range(4 * Z)]
    elif way == "core":
        pairs = [(i, i ^ 1) for i in range(4 * Z)]
    else:
        turn = 4 if way == "+" else -4
        pairs = [(i, (i + turn) % (4 * Z)) for i in range(4 * Z)]
    return lax.ppermute(array, "dp", pairs)


def ring(node_rows, kept_counts, parents, cache_len, cache_kv, norm_gain, w_qkv, b_qkv):
    depth = w_qkv.shape[0]
    group = lax.axis_index("groups")
    index = lax.axis_index("dp")
    z, x, core = index // 4, (index // 2) % 2, index % 2
    half = lax.dynamic_slice(w_qkv, (group * (depth // 2), SPLIT), (depth // 2, w_qkv.shape[1] - SPLIT))
    first = w_qkv[:, :SPLIT]
    tables = tree_tables(parents, cache_len)
    normed, copy = normalize_both(node_rows, move(node_rows, "core"), norm_gain, core, first, tables)
    pieces = {("a", "own"): w_qkv[:, SPLIT:], ("a", "z0"): half, ("b", "own"): first, ("b", "z0"): copy}

    def place(name, chunk):
        if name == "own":
            return 2 * z + x
        side = 1 - group if name[0] == "y" else group
        chip = 2 * ((z - int(name[-1])) % Z) + (1 - x if "x" in name else x)
        return 2 * chip + side if chunk == "a" else chip

    sums = {"a": None, "b": None}
    for line in PLAN:
        if isinstance(line, tuple):
            chunk, names = line
            batch = [(pieces[chunk, name], place(name, chunk)) for name in names]
            copied = first if line == GATE else None
            unread = [pieces["b", name] for name in WAITED.get(line, ())]
            own_sum, other_sum, *copied = accumulate(normed, batch, sums[chunk], copied, unread)
            sums[chunk] = own_sum, other_sum
            if copied:
                pieces["b", "w0"] = copied[0]
        else:
            chunk, way, sent, received = line.split()
            pieces[chunk, received] = move(pieces[chunk, sent], way)

    parts = [part for chunk in "ba" for part in (sums[chunk][0], move(sums[chunk][1], "core"))]
    return attend_sums(parts, b_qkv.reshape(1, -1), tables, kept_counts, cache_len, cache_kv)


def on_device(node_rows, kept_counts, parents, cache_len, cache_kv, norm_gain, w_qkv, b_qkv):
    devices = lax.axis_size("dp")
    if devices == 4 * Z and w_qkv.shape[0] % 512 == 0:
        return ring(node_rows, kept_counts, parents, cache_len, cache_kv, norm_gain, w_qkv, b_qkv)
    weights = lax.all_gather(w_qkv, "dp", axis=0, tiled=True)
    normed = normalize(node_rows, norm_gain)
    tables = tree_tables(parents, cache_len)
    normed, weights, tables = lax.optimization_barrier((normed, weights, tables))
    projected = project(normed, weights, b_qkv)
    return attend(projected, *tables, kept_counts, cache_len, cache_kv)


def solution(mesh):
    return jax.shard_map(
        on_device,
        mesh=mesh,
        in_specs=(
            P(("groups", "dp"), None),
            P(("groups", "dp")),
            P(("groups", "dp"), None),
            P(("groups", "dp")),
            P(("groups", "dp"), None, None, None),
            P(),
            P("dp", None),
            P(),
        ),
        out_specs=P(("groups", "dp"), None),
        check_vma=False,
    )
```
